32 devices in a mesh: node: 8 (over z, x), local: 4 (over y, core).
Axes of the slice: x: 2, y: 2, z: 4, core: 2. Of those that a mesh axis runs over, the one named last changes fastest.
Arguments:
- tokens: bfloat16 [64, 4096], P('node', 'local'), may hold values from -6 to 6
- cotangent: bfloat16 [64, 4096], P('node', 'local'), may hold values from -6 to 6
- expert_ids: int32 [64, 8], P('node'), may hold values from 0 to 7, as said below
- combine_weights: float32 [64, 8], P('node'), may hold values from 0.1 to 1
- w_gate: bfloat16 [8, 4096, 2048], P('node', None, 'local'), may hold values from -0.09375 to 0.09375
- w_up: bfloat16 [8, 4096, 2048], P('node', None, 'local'), may hold values from -0.09375 to 0.09375
- w_down: bfloat16 [8, 2048, 4096], P('node', 'local'), may hold values from -0.125 to 0.125
Outputs:
- layer_out: bfloat16 [64, 4096], P('node', 'local')
- token_grad: bfloat16 [64, 4096], P('node', 'local')
- weight_grad: float32 [64, 8], P('node')
The draws below stay inside these ranges and needn't reach their ends.
Inputs may be any that keep to these rules, and one draw needn't show every extreme that they name: `expert_ids`: each row names 8 different experts, all of them in at most 4 groups of 8 consecutive experts.
All inputs are finite; a program needn't handle non-finite values.
Results may differ from the reference program's by a relative error of at most 0.012.
Values may be sent and summed in bfloat16 or wider, within the bound.
A program may use at most 64 MiB of HBM per device.

```python
import jax
import jax.numpy as jnp
from jax import lax

D = 4096
FF = 2048
TOP = 8
TOPG = 4
EXP_GROUP = 8
TOK_NODE = 8
EXPERTS = 8
TOKENS = 64
SLOT = 8
N_NODE = 8
N_LOCAL = 4


def draw_expert_ids(key, part):
    key = jax.random.fold_in(key, 11)
    groups = EXPERTS // EXP_GROUP
    chosen = min(TOPG, groups)
    key_group, key_bias, key_score = jax.random.split(key, 3)
    group_score = jax.random.randint(key_group, (TOKENS, groups), 0, 4096) * groups + jnp.arange(groups, dtype=jnp.int32)[None, :]
    top_groups = lax.top_k(group_score, chosen)[1].astype(jnp.int32)
    group_of = jnp.arange(EXPERTS, dtype=jnp.int32) // EXP_GROUP
    allowed = jnp.any(group_of[None, None, :] == top_groups[:, :, None], axis=1)
    expert_bias = jax.random.randint(key_bias, (EXPERTS,), 0, 1024)
    noise = jax.random.randint(key_score, (TOKENS, EXPERTS), 0, 1024)
    score = (noise + expert_bias[None, :]) * EXPERTS + jnp.arange(EXPERTS, dtype=jnp.int32)[None, :]
    score = jnp.where(allowed, score, -1)
    return lax.top_k(score, TOP)[1].astype(jnp.int32)


def block_scale(rng, shape, cuts, low, high):
    factor_of, own = 1.0, jax.random.fold_in(rng, 6)
    for axis_at, shards_of in cuts:
        steps = jnp.exp(jax.random.uniform(jax.random.fold_in(own, axis_at), (shards_of,), jnp.float32, low / len(cuts), high / len(cuts)))
        factor_of = factor_of * jnp.repeat(steps, shape[axis_at] // shards_of).reshape([-1 if axis == axis_at else 1 for axis in range(len(shape))])
    return factor_of


def gaussian(rng, extent, spread, reach, pieces=(), kind=jnp.bfloat16):
    drawn = spread * jax.random.normal(rng, extent, jnp.float32)
    if pieces:
        drawn = drawn * block_scale(rng, extent, pieces, -0.22, 0.18)
    return jnp.clip(drawn, -reach, reach).astype(kind)


def setup_inputs(seed: int = 0) -> dict:
    seeds = jax.random.split(jax.random.key(seed), 8)
    return {
        "tokens": gaussian(seeds[0], (TOKENS, D), 1.0, 6.0, ((0, 8), (1, 4))),
        "cotangent": gaussian(seeds[1], (TOKENS, D), 1.0, 6.0, ((0, 8), (1, 4))),
        "expert_ids": draw_expert_ids(jax.random.fold_in(seeds[7], 71), 0),
        "combine_weights": jnp.clip(0.1 + 0.9 * jax.random.uniform(seeds[3], (TOKENS, TOP), jnp.float32) ** block_scale(seeds[3], (TOKENS, TOP), ((0, 8),), -0.2, 0.2), 0.1, 1.0),
        "w_gate": gaussian(seeds[4], (EXPERTS, D, FF), D ** -0.5, 0.09375, ((0, 8), (2, 4))),
        "w_up": gaussian(seeds[5], (EXPERTS, D, FF), D ** -0.5, 0.09375, ((0, 8), (2, 4))),
        "w_down": gaussian(seeds[6], (EXPERTS, FF, D), FF ** -0.5, 0.125, ((0, 8), (1, 4))),
    }


def swiglu_parts(gate_pre, up_pre, grad_hidden):
    sigmoid = jax.nn.sigmoid(gate_pre)
    activated = gate_pre * sigmoid
    hidden = (activated * up_pre).astype(jnp.bfloat16)
    slope = sigmoid * (1.0 + gate_pre * (1.0 - sigmoid))
    grad_gate = (grad_hidden * up_pre * slope).astype(jnp.bfloat16)
    grad_up = (grad_hidden * activated).astype(jnp.bfloat16)
    return hidden, grad_gate, grad_up


def reference(tokens, cotangent, expert_ids, combine_weights, w_gate, w_up, w_down):
    slice_width = FF // N_LOCAL
    row_total = N_NODE * SLOT
    tok_blocks = tokens.reshape(N_NODE, TOK_NODE, D).astype(jnp.float32)
    cot_blocks = cotangent.reshape(N_NODE, TOK_NODE, D).astype(jnp.float32)
    cot_float = cotangent.astype(jnp.float32)
    slot_ids = jnp.arange(SLOT, dtype=jnp.int32)

    def per_expert(carry, inputs):
        out_sum, grad_sum, weight_sum = carry
        weight_gate, weight_up, weight_down, expert = inputs
        matches = (expert_ids == expert).astype(jnp.int32)
        routed = jnp.sum(matches, axis=1).reshape(N_NODE, TOK_NODE)
        position = jnp.cumsum(routed, axis=1) - routed
        kept = routed * (position < SLOT).astype(jnp.int32)
        select = ((kept[:, None, :] == 1) & (position[:, None, :] == slot_ids[None, :, None])).astype(jnp.float32)
        rows_in = jnp.einsum('npi,nid->npd', select, tok_blocks).astype(jnp.bfloat16).reshape(row_total, D)
        rows_grad = jnp.einsum('npi,nid->npd', select, cot_blocks).astype(jnp.bfloat16).reshape(row_total, D)
        gate_pre = jnp.dot(rows_in, weight_gate, preferred_element_type=jnp.float32)
        up_pre = jnp.dot(rows_in, weight_up, preferred_element_type=jnp.float32)
        grad_hidden = jnp.dot(rows_grad, weight_down.T, preferred_element_type=jnp.float32)
        hidden, grad_gate, grad_up = swiglu_parts(gate_pre, up_pre, grad_hidden)
        hidden_split = hidden.reshape(row_total, N_LOCAL, slice_width).astype(jnp.float32)
        down_split = weight_down.reshape(N_LOCAL, slice_width, D).astype(jnp.float32)
        out_part = jnp.einsum('rjf,jfd->jrd', hidden_split, down_split)
        gate_split = weight_gate.reshape(D, N_LOCAL, slice_width).astype(jnp.float32)
        up_split = weight_up.reshape(D, N_LOCAL, slice_width).astype(jnp.float32)
        in_part = jnp.einsum('rjf,djf->jrd', grad_gate.reshape(row_total, N_LOCAL, slice_width).astype(jnp.float32), gate_split)
        in_part = in_part + jnp.einsum('rjf,djf->jrd', grad_up.reshape(row_total, N_LOCAL, slice_width).astype(jnp.float32), up_split)
        out_round = lax.optimization_barrier(out_part.astype(jnp.bfloat16))
        in_round = lax.optimization_barrier(in_part.astype(jnp.bfloat16))
        expert_out = jnp.sum(out_round.astype(jnp.float32), axis=0).astype(jnp.bfloat16)
        expert_in = jnp.sum(in_round.astype(jnp.float32), axis=0).astype(jnp.bfloat16)
        out_tok = jnp.einsum('npi,npd->nid', select, expert_out.reshape(N_NODE, SLOT, D).astype(jnp.float32)).reshape(TOKENS, D)
        in_tok = jnp.einsum('npi,npd->nid', select, expert_in.reshape(N_NODE, SLOT, D).astype(jnp.float32)).reshape(TOKENS, D)
        match_float = matches.astype(jnp.float32)
        gate_here = jnp.sum(combine_weights * match_float, axis=1)
        out_sum = out_sum + gate_here[:, None] * out_tok
        grad_sum = grad_sum + gate_here[:, None] * in_tok
        kept_float = kept.reshape(TOKENS).astype(jnp.float32)
        inner = jnp.sum(cot_float * out_tok, axis=1)
        weight_sum = weight_sum + match_float * (kept_float * inner)[:, None]
        return (out_sum, grad_sum, weight_sum), None

    start = (jnp.zeros((TOKENS, D), jnp.float32), jnp.zeros((TOKENS, D), jnp.float32), jnp.zeros((TOKENS, TOP), jnp.float32))
    expert_range = jnp.arange(EXPERTS, dtype=jnp.int32)
    final, unused = lax.scan(per_expert, start, (w_gate, w_up, w_down, expert_range))
    out_sum, grad_sum, weight_sum = final
    return out_sum.astype(jnp.bfloat16), grad_sum.astype(jnp.bfloat16), weight_sum
```

```python
import functools

import jax
import jax.numpy as jnp
from jax import lax
from jax.experimental import pallas as pl
from jax.experimental.pallas import tpu as pltpu
from jax.sharding import PartitionSpec as P


def swiglu_parts(gate_pre, up_pre, grad_hidden):
    sigmoid = jax.nn.sigmoid(gate_pre)
    activated = gate_pre * sigmoid
    hidden = (activated * up_pre).astype(jnp.bfloat16)
    slope = sigmoid * (1.0 + gate_pre * (1.0 - sigmoid))
    grad_gate = (grad_hidden * up_pre * slope).astype(jnp.bfloat16)
    grad_up = (grad_hidden * activated).astype(jnp.bfloat16)
    return (hidden, grad_gate, grad_up)


def general_body(tokens, cotangent, expert_ids, combine_weights, w_gate, w_up, w_down):
    experts = lax.axis_size("node")
    node_tokens, width_local = tokens.shape
    top_count = expert_ids.shape[1]
    capacity = min(node_tokens, (3 * node_tokens * top_count + 2 * experts - 1) // (2 * experts))
    row_total = experts * capacity
    matches = (expert_ids[:, :, None] == lax.iota(jnp.int32, experts)[None, None, :]).astype(
        jnp.int32
    )
    routed = jnp.sum(matches, axis=1)
    position = jnp.cumsum(routed, axis=0) - routed
    kept = routed * (position < capacity).astype(jnp.int32)
    slot_ids = lax.iota(jnp.int32, capacity)
    select_mask = (kept.T[:, None, :] == 1) & (position.T[:, None, :] == slot_ids[None, :, None])
    select_float = select_mask.astype(jnp.float32)
    select_half = select_mask.astype(jnp.bfloat16)
    send_tok = jnp.einsum(
        "epi,id->epd", select_half, tokens, preferred_element_type=jnp.float32
    ).astype(jnp.bfloat16)
    send_cot = jnp.einsum(
        "epi,id->epd", select_half, cotangent, preferred_element_type=jnp.float32
    ).astype(jnp.bfloat16)
    recv_tok, recv_cot = (
        lax.all_to_all(send_tok, "node", split_axis=0, concat_axis=0, tiled=True),
        lax.all_to_all(send_cot, "node", split_axis=0, concat_axis=0, tiled=True),
    )
    weight_gate = w_gate[0]
    weight_up = w_up[0]
    weight_down = w_down[0]
    full_tok, full_cot = (
        lax.all_gather(recv_tok, "local", axis=2, tiled=True),
        lax.all_gather(recv_cot, "local", axis=2, tiled=True),
    )
    flat_tok = full_tok.reshape(row_total, -1)
    flat_cot = full_cot.reshape(row_total, -1)
    gate_pre = jnp.dot(flat_tok, weight_gate, preferred_element_type=jnp.float32)
    up_pre = jnp.dot(flat_tok, weight_up, preferred_element_type=jnp.float32)
    grad_hidden = jnp.einsum("rd,fd->rf", flat_cot, weight_down, preferred_element_type=jnp.float32)
    hidden, grad_gate, grad_up = swiglu_parts(gate_pre, up_pre, grad_hidden)
    output_part = jnp.einsum("fc,rf->cr", weight_down, hidden, preferred_element_type=jnp.float32)
    input_part = jnp.einsum("cf,rf->cr", weight_gate, grad_gate, preferred_element_type=jnp.float32)
    input_part = input_part + jnp.einsum(
        "cf,rf->cr", weight_up, grad_up, preferred_element_type=jnp.float32
    )
    summed = lax.psum_scatter(
        jnp.concatenate([output_part, input_part], axis=1).astype(jnp.bfloat16),
        "local",
        scatter_dimension=0,
        tiled=True,
    )
    outgoing = summed.reshape(width_local, 2, experts, capacity)
    returned = lax.all_to_all(outgoing, "node", split_axis=2, concat_axis=2, tiled=True)
    returned_float = returned.astype(jnp.float32)
    gate_table = jnp.sum(combine_weights[:, :, None] * matches.astype(jnp.float32), axis=1)
    weighted = select_float * gate_table.T[:, None, :]
    layer_out = jnp.einsum("epi,cep->ic", weighted, returned_float[:, 0]).astype(jnp.bfloat16)
    token_grad = jnp.einsum("epi,cep->ic", weighted, returned_float[:, 1]).astype(jnp.bfloat16)
    slot_inner = jnp.einsum("cep,epc->ep", returned_float[:, 0], send_cot.astype(jnp.float32))
    inner = jnp.einsum("epi,ep->ie", select_float, slot_inner)
    partial_grad = jnp.sum(inner[:, None, :] * matches.astype(jnp.float32), axis=2)
    weight_grad = lax.psum(partial_grad, "local")
    return (layer_out, token_grad, weight_grad)


MESH = pl.DeviceIdType.MESH
NT = (((1,), (1,)), ((), ()))
NN = (((1,), (0,)), ((), ()))


def mm(a, b, dims):
    return lax.dot_general(a, b, dims, preferred_element_type=jnp.float32)


def fused_kernel(
    nodes,
    tok_ref,
    cot_ref,
    ids_ref,
    cw_ref,
    wg_hbm,
    wu_hbm,
    wd_hbm,
    lo_ref,
    tg_ref,
    wgrad_ref,
    wg_v,
    wu_v,
    wd_v,
    xb,
    gt,
    rl,
    rn_s,
    rn,
    mate_s,
    mate_r,
    y_s,
    y_r,
    n_s,
    n_r,
    part,
    w_sem,
    xs_sem,
    xr_sem,
    gs_sem,
    gr_sem,
    ls_sem,
    lr_sem,
    ns_sem,
    nr_sem,
    ms_sem,
    mr_sem,
    ys_sem,
    yr_sem,
    os_sem,
    or_sem,
):
    me = lax.axis_index("node")
    l = lax.axis_index("local")
    core = lax.rem(l, 2)
    mate = l + 1 - 2 * core
    ymate = lax.rem(l + 2, 4)
    diag = lax.rem(mate + 2, 4)
    order = (l, mate, ymate, diag)
    toks, width = tok_ref.shape
    rows = nodes * toks

    def peer(d):
        return lax.rem(me + d, nodes)

    def source(d):
        return lax.rem(me - d + nodes, nodes)

    w_copies = []
    for j, c in enumerate(order):
        cols = pl.ds(pl.multiple_of(c * width, width), width)
        group = (
            pltpu.make_async_copy(wg_hbm.at[0, cols, :], wg_v.at[c], w_sem.at[0, j]),
            pltpu.make_async_copy(wu_hbm.at[0, cols, :], wu_v.at[c], w_sem.at[1, j]),
            pltpu.make_async_copy(wd_hbm.at[0, :, cols], wd_v.at[c], w_sem.at[2, j]),
        )
        for copy in group:
            copy.start()
        w_copies.append(group)

    barrier = pltpu.get_barrier_semaphore()
    for d in range(1, nodes):
        pl.semaphore_signal(barrier, inc=1, device_id=(peer(d), l), device_id_type=MESH)
    for c in (mate, ymate, diag):
        pl.semaphore_signal(barrier, inc=1, device_id=(me, c), device_id_type=MESH)

    xb[l, me] = jnp.concatenate(
        [tok_ref[...].astype(jnp.float32), cot_ref[...].astype(jnp.float32)], axis=0
    ).astype(jnp.bfloat16)
    ids = ids_ref[...]
    lanes = lax.broadcasted_iota(jnp.int32, (toks, 128), 1)
    table = jnp.zeros((toks, 128), jnp.float32)
    for k in range(ids.shape[1]):
        table = table + jnp.where(lanes == ids[:, k : k + 1], cw_ref[:, k : k + 1], 0.0)
    gt[me] = table

    pl.semaphore_wait(barrier, nodes + 2)

    sends = []

    def send(src, dst, ssem, rsem, device):
        copy = pltpu.make_async_remote_copy(
            src_ref=src,
            dst_ref=dst,
            send_sem=ssem,
            recv_sem=rsem,
            device_id=device,
            device_id_type=MESH,
        )
        copy.start()
        sends.append(copy)
        return copy

    x_node = [None]
    g_node = [None]
    for d in range(1, nodes):
        x_node.append(
            send(xb.at[l, me], xb.at[l, me], xs_sem.at[0, d], xr_sem.at[0, d], (peer(d), l))
        )
    x_mate, x_y, x_diag = [], [], []

    def onward(d):
        block = xb.at[l, source(d)]
        x_y.append(send(block, block, xs_sem.at[1, d], xr_sem.at[1, d], (me, ymate)))
        x_mate.append(send(block, block, xs_sem.at[2, d], xr_sem.at[2, d], (me, mate)))

    def relay(d):
        x_y[d].wait_recv()
        block = xb.at[ymate, source(d)]
        x_diag.append(send(block, block, xs_sem.at[3, d], xr_sem.at[3, d], (me, mate)))

    onward(0)
    for d in range(1, nodes):
        g_node.append(send(gt.at[me], gt.at[me], gs_sem.at[d], gr_sem.at[d], (peer(d), l)))
    for d in range(1, nodes):
        x_node[d].wait_recv()
        onward(d)
        relay(d - 1)
    relay(nodes - 1)

    gate_pre = up_pre = grad_hidden = None
    for j, c in enumerate(order):
        for copy in w_copies[j]:
            copy.wait()
        if j == 1:
            for copy in x_mate:
                copy.wait_recv()
        if j == 3:
            for copy in x_diag:
                copy.wait_recv()
        both = xb[c].astype(jnp.float32).reshape(nodes, 2, toks, width)
        tok = both[:, 0].reshape(rows, width).astype(jnp.bfloat16)
        cot = both[:, 1].reshape(rows, width).astype(jnp.bfloat16)
        a = mm(tok, wg_v[c], NN)
        b = mm(tok, wu_v[c], NN)
        g = mm(cot, wd_v[c], NT)
        if j == 0:
            gate_pre, up_pre, grad_hidden = a, b, g
        else:
            gate_pre, up_pre, grad_hidden = gate_pre + a, up_pre + b, grad_hidden + g

    for copy in g_node[1:]:
        copy.wait_recv()
    lanes3 = lax.broadcasted_iota(jnp.int32, (nodes, toks, 128), 2)
    scale = jnp.sum(jnp.where(lanes3 == me, gt[...], 0.0), axis=2, keepdims=True).reshape(rows, 1)
    sigmoid = jax.nn.sigmoid(gate_pre)
    activated = gate_pre * sigmoid
    hidden = activated * up_pre
    slope = sigmoid * (1.0 + gate_pre * (1.0 - sigmoid))
    inner = jnp.sum(hidden * grad_hidden, axis=1, keepdims=True).reshape(nodes, toks, 1)
    nodes3 = lax.broadcasted_iota(jnp.int32, (nodes, toks, 128), 0)
    rl[l] = jnp.sum(jnp.where(lanes3 == nodes3, inner, 0.0), axis=0)
    r_local = []
    for j, c in enumerate((mate, ymate, diag)):
        r_local.append(send(rl.at[l], rl.at[l], ls_sem.at[j], lr_sem.at[j], (me, c)))
    scaled = grad_hidden * scale
    hid = (hidden * scale).astype(jnp.bfloat16)
    ggate = (scaled * up_pre * slope).astype(jnp.bfloat16)
    gup = (scaled * activated).astype(jnp.bfloat16)

    def partial(c):
        out = mm(hid, wd_v[c], NN).reshape(nodes, toks, width)
        into = (mm(ggate, wg_v[c], NT) + mm(gup, wu_v[c], NT)).reshape(nodes, toks, width)
        return jnp.concatenate([out, into], axis=1)

    def to_mate(i, c):
        mate_s[i] = partial(c).astype(jnp.bfloat16)
        return send(mate_s.at[i], mate_r.at[i], ms_sem.at[i], mr_sem.at[i], (me, mate))

    first = to_mate(0, diag)
    part[...] = partial(ymate)
    first.wait_recv()
    y_s[...] = (part[...] + mate_r[0].astype(jnp.float32)).astype(jnp.bfloat16)
    turns = list(range(1, nodes)) + [0]
    y_copies = {}
    for d in turns:
        n = peer(d)
        y_copies[d] = send(y_s.at[n], y_r.at[n], ys_sem.at[d], yr_sem.at[d], (me, ymate))
    second = to_mate(1, mate)
    part[...] = partial(l)

    for copy in r_local:
        copy.wait_recv()
    r_sum = rl[0] + rl[1] + rl[2] + rl[3]
    r_node = []
    for d in turns:
        n = peer(d)
        column = jnp.sum(jnp.where(lanes == n, r_sum, 0.0), axis=1, keepdims=True)
        rn_s[d] = jnp.where(lanes == me, column, 0.0)
        if d:
            r_node.append(send(rn_s.at[d], rn.at[me], ns_sem.at[d], nr_sem.at[d], (n, l)))

    second.wait_recv()
    o_node = []
    total = None
    for d in turns:
        n = peer(d)
        y_copies[d].wait_recv()
        value = part[n] + mate_r[1, n].astype(jnp.float32) + y_r[n].astype(jnp.float32)
        if d:
            n_s[d] = value.astype(jnp.bfloat16)
            o_node.append(send(n_s.at[d], n_r.at[me], os_sem.at[d], or_sem.at[d], (n, l)))
        else:
            total = value
    r_total = rn_s[0]
    for i, d in enumerate(range(1, nodes)):
        r_node[i].wait_recv()
        r_total = r_total + rn[source(d)]
    answer = jnp.zeros(ids.shape, jnp.float32)
    slots = lax.broadcasted_iota(jnp.int32, ids.shape, 1)
    for k in range(ids.shape[1]):
        value = jnp.sum(jnp.where(lanes == ids[:, k : k + 1], r_total, 0.0), axis=1, keepdims=True)
        answer = answer + jnp.where(slots == k, value, 0.0)
    wgrad_ref[...] = answer
    for i, d in enumerate(range(1, nodes)):
        o_node[i].wait_recv()
        total = total + n_r[source(d)].astype(jnp.float32)
    lo_ref[...] = total[:toks].astype(jnp.bfloat16)
    tg_ref[...] = total[toks:].astype(jnp.bfloat16)
    for copy in sends:
        copy.wait_send()


def fused_body(tokens, cotangent, expert_ids, combine_weights, w_gate, w_up, w_down):
    nodes = lax.axis_size("node")
    toks, width = tokens.shape
    units = w_gate.shape[2]
    half, single = jnp.bfloat16, jnp.float32
    block = (nodes, 2 * toks, width)
    dma = pltpu.SemaphoreType.DMA
    vmem = pl.BlockSpec(memory_space=pltpu.VMEM)
    hbm = pl.BlockSpec(memory_space=pl.ANY)
    return pl.pallas_call(
        functools.partial(fused_kernel, nodes),
        out_shape=(
            jax.ShapeDtypeStruct((toks, width), half),
            jax.ShapeDtypeStruct((toks, width), half),
            jax.ShapeDtypeStruct(expert_ids.shape, single),
        ),
        in_specs=[vmem] * 4 + [hbm] * 3,
        out_specs=(vmem, vmem, vmem),
        scratch_shapes=[
            pltpu.VMEM((4, width, units), half),
            pltpu.VMEM((4, width, units), half),
            pltpu.VMEM((4, units, width), half),
            pltpu.VMEM((4,) + block, half),
            pltpu.VMEM((nodes, toks, 128), single),
            pltpu.VMEM((4, toks, 128), single),
            pltpu.VMEM((nodes, toks, 128), single),
            pltpu.VMEM((nodes, toks, 128), single),
            pltpu.VMEM((2,) + block, half),
            pltpu.VMEM((2,) + block, half),
            pltpu.VMEM(block, half),
            pltpu.VMEM(block, half),
            pltpu.VMEM(block, half),
            pltpu.VMEM(block, half),
            pltpu.VMEM(block, single),
            dma((3, 4)),
            dma((4, nodes)),
            dma((4, nodes)),
            dma((nodes,)),
            dma((nodes,)),
            dma((3,)),
            dma((3,)),
            dma((nodes,)),
            dma((nodes,)),
            dma((2,)),
            dma((2,)),
            dma((nodes,)),
            dma((nodes,)),
            dma((nodes,)),
            dma((nodes,)),
        ],
        compiler_params=pltpu.CompilerParams(
            collective_id=0, has_side_effects=True, vmem_limit_bytes=44 * 1024 * 1024
        ),
    )(tokens, cotangent, expert_ids, combine_weights, w_gate, w_up, w_down)


def body(tokens, cotangent, expert_ids, combine_weights, w_gate, w_up, w_down):
    experts = lax.axis_size("node")
    node_tokens = tokens.shape[0]
    top_count = expert_ids.shape[1]
    capacity = min(node_tokens, (3 * node_tokens * top_count + 2 * experts - 1) // (2 * experts))
    whole = capacity == node_tokens and node_tokens == 8 and experts <= 128
    chosen = fused_body if whole and lax.axis_size("local") == 4 else general_body
    return chosen(tokens, cotangent, expert_ids, combine_weights, w_gate, w_up, w_down)


def solution(mesh):
    in_specs = (
        P("node", "local"),
        P("node", "local"),
        P("node", None),
        P("node", None),
        P("node", None, "local"),
        P("node", None, "local"),
        P("node", "local", None),
    )
    out_specs = (P("node", "local"), P("node", "local"), P("node", None))
    return jax.shard_map(body, mesh=mesh, in_specs=in_specs, out_specs=out_specs, check_vma=False)
```

```python
import functools

import jax
import jax.numpy as jnp
from jax import lax
from jax.experimental import pallas as pl
from jax.experimental.pallas import tpu as pltpu
from jax.sharding import PartitionSpec as P


def swiglu_parts(gate_pre, up_pre, grad_hidden):
    sigmoid = jax.nn.sigmoid(gate_pre)
    activated = gate_pre * sigmoid
    hidden = (activated * up_pre).astype(jnp.bfloat16)
    slope = sigmoid * (1.0 + gate_pre * (1.0 - sigmoid))
    grad_gate = (grad_hidden * up_pre * slope).astype(jnp.bfloat16)
    grad_up = (grad_hidden * activated).astype(jnp.bfloat16)
    return (hidden, grad_gate, grad_up)


def general_body(tokens, cotangent, expert_ids, combine_weights, w_gate, w_up, w_down):
    experts = lax.axis_size("node")
    node_tokens, width_local = tokens.shape
    top_count = expert_ids.shape[1]
    capacity = min(node_tokens, (3 * node_tokens * top_count + 2 * experts - 1) // (2 * experts))
    row_total = experts * capacity
    matches = (expert_ids[:, :, None] == lax.iota(jnp.int32, experts)[None, None, :]).astype(
        jnp.int32
    )
    routed = jnp.sum(matches, axis=1)
    position = jnp.cumsum(routed, axis=0) - routed
    kept = routed * (position < capacity).astype(jnp.int32)
    slot_ids = lax.iota(jnp.int32, capacity)
    select_mask = (kept.T[:, None, :] == 1) & (position.T[:, None, :] == slot_ids[None, :, None])
    select_float = select_mask.astype(jnp.float32)
    select_half = select_mask.astype(jnp.bfloat16)
    send_tok = jnp.einsum(
        "epi,id->epd", select_half, tokens, preferred_element_type=jnp.float32
    ).astype(jnp.bfloat16)
    send_cot = jnp.einsum(
        "epi,id->epd", select_half, cotangent, preferred_element_type=jnp.float32
    ).astype(jnp.bfloat16)
    recv_tok, recv_cot = (
        lax.all_to_all(send_tok, "node", split_axis=0, concat_axis=0, tiled=True),
        lax.all_to_all(send_cot, "node", split_axis=0, concat_axis=0, tiled=True),
    )
    weight_gate = w_gate[0]
    weight_up = w_up[0]
    weight_down = w_down[0]
    full_tok, full_cot = (
        lax.all_gather(recv_tok, "local", axis=2, tiled=True),
        lax.all_gather(recv_cot, "local", axis=2, tiled=True),
    )
    flat_tok = full_tok.reshape(row_total, -1)
    flat_cot = full_cot.reshape(row_total, -1)
    gate_pre = jnp.dot(flat_tok, weight_gate, preferred_element_type=jnp.float32)
    up_pre = jnp.dot(flat_tok, weight_up, preferred_element_type=jnp.float32)
    grad_hidden = jnp.einsum("rd,fd->rf", flat_cot, weight_down, preferred_element_type=jnp.float32)
    hidden, grad_gate, grad_up = swiglu_parts(gate_pre, up_pre, grad_hidden)
    output_part = jnp.einsum("fc,rf->cr", weight_down, hidden, preferred_element_type=jnp.float32)
    input_part = jnp.einsum("cf,rf->cr", weight_gate, grad_gate, preferred_element_type=jnp.float32)
    input_part = input_part + jnp.einsum(
        "cf,rf->cr", weight_up, grad_up, preferred_element_type=jnp.float32
    )
    summed = lax.psum_scatter(
        jnp.concatenate([output_part, input_part], axis=1).astype(jnp.bfloat16),
        "local",
        scatter_dimension=0,
        tiled=True,
    )
    outgoing = summed.reshape(width_local, 2, experts, capacity)
    returned = lax.all_to_all(outgoing, "node", split_axis=2, concat_axis=2, tiled=True)
    returned_float = returned.astype(jnp.float32)
    gate_table = jnp.sum(combine_weights[:, :, None] * matches.astype(jnp.float32), axis=1)
    weighted = select_float * gate_table.T[:, None, :]
    layer_out = jnp.einsum("epi,cep->ic", weighted, returned_float[:, 0]).astype(jnp.bfloat16)
    token_grad = jnp.einsum("epi,cep->ic", weighted, returned_float[:, 1]).astype(jnp.bfloat16)
    slot_inner = jnp.einsum("cep,epc->ep", returned_float[:, 0], send_cot.astype(jnp.float32))
    inner = jnp.einsum("epi,ep->ie", select_float, slot_inner)
    partial_grad = jnp.sum(inner[:, None, :] * matches.astype(jnp.float32), axis=2)
    weight_grad = lax.psum(partial_grad, "local")
    return (layer_out, token_grad, weight_grad)


MESH = pl.DeviceIdType.MESH
NT = (((1,), (1,)), ((), ()))
NN = (((1,), (0,)), ((), ()))


def mm(a, b, dims):
    return lax.dot_general(a, b, dims, preferred_element_type=jnp.float32)


def fused_kernel(
    nodes,
    tok_hbm,
    cot_hbm,
    ids_hbm,
    cw_hbm,
    wg_hbm,
    wu_hbm,
    wd_hbm,
    lo_ref,
    tg_ref,
    wgrad_ref,
    tok_ref,
    cot_ref,
    ids_ref,
    cw_ref,
    wg_v,
    wu_v,
    wd_v,
    xb,
    gt,
    rl,
    rn_s,
    rn,
    mate_s,
    mate_r,
    y_s,
    y_r,
    n_s,
    n_r,
    part,
    in_sem,
    w_sem,
    xs_sem,
    xr_sem,
    gs_sem,
    gr_sem,
    ls_sem,
    lr_sem,
    ns_sem,
    nr_sem,
    ms_sem,
    mr_sem,
    ys_sem,
    yr_sem,
    os_sem,
    or_sem,
):
    me = lax.axis_index("node")
    l = lax.axis_index("local")
    core = lax.rem(l, 2)
    mate = l + 1 - 2 * core
    ymate = lax.rem(l + 2, 4)
    diag = lax.rem(mate + 2, 4)
    order = (l, mate, ymate, diag)
    toks, width = tok_ref.shape
    rows = nodes * toks

    def peer(d):
        return lax.rem(me + d, nodes)

    def source(d):
        return lax.rem(me - d + nodes, nodes)

    in_copies = []
    in_pairs = ((tok_hbm, tok_ref), (cot_hbm, cot_ref), (ids_hbm, ids_ref), (cw_hbm, cw_ref))
    for j, (far, near) in enumerate(in_pairs):
        in_copies.append(pltpu.make_async_copy(far, near, in_sem.at[j]))
        in_copies[j].start()

    barrier = pltpu.get_barrier_semaphore()
    for d in range(1, nodes):
        pl.semaphore_signal(barrier, inc=1, device_id=(peer(d), l), device_id_type=MESH)
    for c in (mate, ymate, diag):
        pl.semaphore_signal(barrier, inc=1, device_id=(me, c), device_id_type=MESH)

    w_copies = []
    for j, c in enumerate(order):
        cols = pl.ds(pl.multiple_of(c * width, width), width)
        group = (
            pltpu.make_async_copy(wg_hbm.at[0, cols, :], wg_v.at[c], w_sem.at[0, j]),
            pltpu.make_async_copy(wu_hbm.at[0, cols, :], wu_v.at[c], w_sem.at[1, j]),
            pltpu.make_async_copy(wd_hbm.at[0, :, cols], wd_v.at[c], w_sem.at[2, j]),
        )
        for copy in group:
            copy.start()
        w_copies.append(group)

    for copy in in_copies:
        copy.wait()
    xb[l, me] = jnp.concatenate(
        [tok_ref[...].astype(jnp.float32), cot_ref[...].astype(jnp.float32)], axis=0
    ).astype(jnp.bfloat16)
    ids = ids_ref[...]
    lanes = lax.broadcasted_iota(jnp.int32, (toks, 128), 1)
    table = jnp.zeros((toks, 128), jnp.float32)
    for k in range(ids.shape[1]):
        table = table + jnp.where(lanes == ids[:, k : k + 1], cw_ref[:, k : k + 1], 0.0)
    gt[me] = table

    pl.semaphore_wait(barrier, nodes + 2)

    sends = []

    def send(src, dst, ssem, rsem, device):
        copy = pltpu.make_async_remote_copy(
            src_ref=src,
            dst_ref=dst,
            send_sem=ssem,
            recv_sem=rsem,
            device_id=device,
            device_id_type=MESH,
        )
        copy.start()
        sends.append(copy)
        return copy

    x_node = [None]
    g_node = [None]
    for d in range(1, nodes):
        x_node.append(
            send(xb.at[l, me], xb.at[l, me], xs_sem.at[0, d], xr_sem.at[0, d], (peer(d), l))
        )
    x_mate, x_y, x_diag = [], [], []

    def onward(d):
        block = xb.at[l, source(d)]
        x_y.append(send(block, block, xs_sem.at[1, d], xr_sem.at[1, d], (me, ymate)))
        x_mate.append(send(block, block, xs_sem.at[2, d], xr_sem.at[2, d], (me, mate)))

    def relay(d):
        x_y[d].wait_recv()
        block = xb.at[ymate, source(d)]
        x_diag.append(send(block, block, xs_sem.at[3, d], xr_sem.at[3, d], (me, mate)))

    onward(0)
    for d in range(1, nodes):
        g_node.append(send(gt.at[me], gt.at[me], gs_sem.at[d], gr_sem.at[d], (peer(d), l)))
    for d in range(1, nodes):
        x_node[d].wait_recv()
        onward(d)

    gate_pre = up_pre = grad_hidden = None
    for j, c in enumerate(order):
        for copy in w_copies[j]:
            copy.wait()
        if j == 1:
            for d in range(nodes):
                relay(d)
            for copy in x_mate:
                copy.wait_recv()
        if j == 3:
            for copy in x_diag:
                copy.wait_recv()
        both = xb[c].astype(jnp.float32).reshape(nodes, 2, toks, width)
        tok = both[:, 0].reshape(rows, width).astype(jnp.bfloat16)
        cot = both[:, 1].reshape(rows, width).astype(jnp.bfloat16)
        a = mm(tok, wg_v[c], NN)
        b = mm(tok, wu_v[c], NN)
        g = mm(cot, wd_v[c], NT)
        if j == 0:
            gate_pre, up_pre, grad_hidden = a, b, g
        else:
            gate_pre, up_pre, grad_hidden = gate_pre + a, up_pre + b, grad_hidden + g

    for copy in g_node[1:]:
        copy.wait_recv()
    lanes3 = lax.broadcasted_iota(jnp.int32, (nodes, toks, 128), 2)
    scale = jnp.sum(jnp.where(lanes3 == me, gt[...], 0.0), axis=2, keepdims=True).reshape(rows, 1)
    sigmoid = jax.nn.sigmoid(gate_pre)
    activated = gate_pre * sigmoid
    hidden = activated * up_pre
    slope = sigmoid * (1.0 + gate_pre * (1.0 - sigmoid))
    inner = jnp.sum(hidden * grad_hidden, axis=1, keepdims=True).reshape(nodes, toks, 1)
    nodes3 = lax.broadcasted_iota(jnp.int32, (nodes, toks, 128), 0)
    rl[l] = jnp.sum(jnp.where(lanes3 == nodes3, inner, 0.0), axis=0)
    r_local = []
    for j, c in enumerate((mate, ymate, diag)):
        r_local.append(send(rl.at[l], rl.at[l], ls_sem.at[j], lr_sem.at[j], (me, c)))
    scaled = grad_hidden * scale
    hid = (hidden * scale).astype(jnp.bfloat16)
    ggate = (scaled * up_pre * slope).astype(jnp.bfloat16)
    gup = (scaled * activated).astype(jnp.bfloat16)

    def partial(c):
        out = mm(hid, wd_v[c], NN).reshape(nodes, toks, width)
        into = (mm(ggate, wg_v[c], NT) + mm(gup, wu_v[c], NT)).reshape(nodes, toks, width)
        return jnp.concatenate([out, into], axis=1)

    def to_mate(i, c):
        mate_s[i] = partial(c).astype(jnp.bfloat16)
        return send(mate_s.at[i], mate_r.at[i], ms_sem.at[i], mr_sem.at[i], (me, mate))

    first = to_mate(0, diag)
    part[...] = partial(ymate)
    first.wait_recv()
    y_s[...] = (part[...] + mate_r[0].astype(jnp.float32)).astype(jnp.bfloat16)
    turns = list(range(1, nodes)) + [0]
    y_copies = {}
    for d in turns:
        n = peer(d)
        y_copies[d] = send(y_s.at[n], y_r.at[n], ys_sem.at[d], yr_sem.at[d], (me, ymate))
    second = to_mate(1, mate)
    part[...] = partial(l)

    for copy in r_local:
        copy.wait_recv()
    r_sum = rl[0] + rl[1] + rl[2] + rl[3]
    r_node = []
    for d in turns:
        n = peer(d)
        column = jnp.sum(jnp.where(lanes == n, r_sum, 0.0), axis=1, keepdims=True)
        rn_s[d] = jnp.where(lanes == me, column, 0.0)
        if d:
            r_node.append(send(rn_s.at[d], rn.at[me], ns_sem.at[d], nr_sem.at[d], (n, l)))

    second.wait_recv()
    o_node = []
    total = None
    for d in turns:
        n = peer(d)
        y_copies[d].wait_recv()
        value = part[n] + mate_r[1, n].astype(jnp.float32) + y_r[n].astype(jnp.float32)
        if d:
            n_s[d] = value.astype(jnp.bfloat16)
            o_node.append(send(n_s.at[d], n_r.at[me], os_sem.at[d], or_sem.at[d], (n, l)))
        else:
            total = value
    r_total = rn_s[0]
    for i, d in enumerate(range(1, nodes)):
        r_node[i].wait_recv()
        r_total = r_total + rn[source(d)]
    answer = jnp.zeros(ids.shape, jnp.float32)
    slots = lax.broadcasted_iota(jnp.int32, ids.shape, 1)
    for k in range(ids.shape[1]):
        value = jnp.sum(jnp.where(lanes == ids[:, k : k + 1], r_total, 0.0), axis=1, keepdims=True)
        answer = answer + jnp.where(slots == k, value, 0.0)
    wgrad_ref[...] = answer
    for i, d in enumerate(range(1, nodes)):
        o_node[i].wait_recv()
        total = total + n_r[source(d)].astype(jnp.float32)
    lo_ref[...] = total[:toks].astype(jnp.bfloat16)
    tg_ref[...] = total[toks:].astype(jnp.bfloat16)
    for copy in sends:
        copy.wait_send()


def write_kernel(a_ref, b_ref, c_ref, x_ref, y_ref, z_ref):
    x_ref[...] = a_ref[...]
    y_ref[...] = b_ref[...]
    z_ref[...] = c_ref[...]


def fused_body(tokens, cotangent, expert_ids, combine_weights, w_gate, w_up, w_down):
    nodes = lax.axis_size("node")
    toks, width = tokens.shape
    units = w_gate.shape[2]
    half, single = jnp.bfloat16, jnp.float32
    block = (nodes, 2 * toks, width)
    dma = pltpu.SemaphoreType.DMA
    vmem = pl.BlockSpec(memory_space=pltpu.VMEM)
    hbm = pl.BlockSpec(memory_space=pltpu.HBM)
    shapes = (
        jax.ShapeDtypeStruct((toks, width), half),
        jax.ShapeDtypeStruct((toks, width), half),
        jax.ShapeDtypeStruct(expert_ids.shape, single),
    )
    results = pl.pallas_call(
        functools.partial(fused_kernel, nodes),
        out_shape=shapes,
        in_specs=[hbm] * 7,
        out_specs=(vmem, vmem, vmem),
        scratch_shapes=[
            pltpu.VMEM((toks, width), half),
            pltpu.VMEM((toks, width), half),
            pltpu.VMEM(expert_ids.shape, jnp.int32),
            pltpu.VMEM(combine_weights.shape, single),
            pltpu.VMEM((4, width, units), half),
            pltpu.VMEM((4, width, units), half),
            pltpu.VMEM((4, units, width), half),
            pltpu.VMEM((4,) + block, half),
            pltpu.VMEM((nodes, toks, 128), single),
            pltpu.VMEM((4, toks, 128), single),
            pltpu.VMEM((nodes, toks, 128), single),
            pltpu.VMEM((nodes, toks, 128), single),
            pltpu.VMEM((2,) + block, half),
            pltpu.VMEM((2,) + block, half),
            pltpu.VMEM(block, half),
            pltpu.VMEM(block, half),
            pltpu.VMEM(block, half),
            pltpu.VMEM(block, half),
            pltpu.VMEM(block, single),
            dma((4,)),
            dma((3, 4)),
            dma((4, nodes)),
            dma((4, nodes)),
            dma((nodes,)),
            dma((nodes,)),
            dma((3,)),
            dma((3,)),
            dma((nodes,)),
            dma((nodes,)),
            dma((2,)),
            dma((2,)),
            dma((nodes,)),
            dma((nodes,)),
            dma((nodes,)),
            dma((nodes,)),
        ],
        compiler_params=pltpu.CompilerParams(
            collective_id=0, has_side_effects=True, vmem_limit_bytes=62 * 1024 * 1024
        ),
    )(tokens, cotangent, expert_ids, combine_weights, w_gate, w_up, w_down)
    return pl.pallas_call(
        write_kernel, out_shape=shapes, in_specs=[vmem] * 3, out_specs=(vmem, vmem, vmem)
    )(*results)


def body(tokens, cotangent, expert_ids, combine_weights, w_gate, w_up, w_down):
    experts = lax.axis_size("node")
    node_tokens = tokens.shape[0]
    top_count = expert_ids.shape[1]
    capacity = min(node_tokens, (3 * node_tokens * top_count + 2 * experts - 1) // (2 * experts))
    whole = capacity == node_tokens and node_tokens == 8 and experts <= 128
    chosen = fused_body if whole and lax.axis_size("local") == 4 else general_body
    return chosen(tokens, cotangent, expert_ids, combine_weights, w_gate, w_up, w_down)


def solution(mesh):
    in_specs = (
        P("node", "local"),
        P("node", "local"),
        P("node", None),
        P("node", None),
        P("node", None, "local"),
        P("node", None, "local"),
        P("node", "local", None),
    )
    out_specs = (P("node", "local"), P("node", "local"), P("node", None))
    return jax.shard_map(body, mesh=mesh, in_specs=in_specs, out_specs=out_specs, check_vma=False)
```

```python
import functools

import jax
import jax.numpy as jnp
from jax import lax
from jax.experimental import pallas as pl
from jax.experimental.pallas import tpu as pltpu
from jax.sharding import PartitionSpec as P


def swiglu_parts(gate_pre, up_pre, grad_hidden):
    sigmoid = jax.nn.sigmoid(gate_pre)
    activated = gate_pre * sigmoid
    hidden = (activated * up_pre).astype(jnp.bfloat16)
    slope = sigmoid * (1.0 + gate_pre * (1.0 - sigmoid))
    grad_gate = (grad_hidden * up_pre * slope).astype(jnp.bfloat16)
    grad_up = (grad_hidden * activated).astype(jnp.bfloat16)
    return (hidden, grad_gate, grad_up)


def general_body(tokens, cotangent, expert_ids, combine_weights, w_gate, w_up, w_down):
    experts = lax.axis_size("node")
    node_tokens, width_local = tokens.shape
    top_count = expert_ids.shape[1]
    capacity = min(node_tokens, (3 * node_tokens * top_count + 2 * experts - 1) // (2 * experts))
    row_total = experts * capacity
    matches = (expert_ids[:, :, None] == lax.iota(jnp.int32, experts)[None, None, :]).astype(
        jnp.int32
    )
    routed = jnp.sum(matches, axis=1)
    position = jnp.cumsum(routed, axis=0) - routed
    kept = routed * (position < capacity).astype(jnp.int32)
    slot_ids = lax.iota(jnp.int32, capacity)
    select_mask = (kept.T[:, None, :] == 1) & (position.T[:, None, :] == slot_ids[None, :, None])
    select_float = select_mask.astype(jnp.float32)
    select_half = select_mask.astype(jnp.bfloat16)
    send_tok = jnp.einsum(
        "epi,id->epd", select_half, tokens, preferred_element_type=jnp.float32
    ).astype(jnp.bfloat16)
    send_cot = jnp.einsum(
        "epi,id->epd", select_half, cotangent, preferred_element_type=jnp.float32
    ).astype(jnp.bfloat16)
    recv_tok, recv_cot = (
        lax.all_to_all(send_tok, "node", split_axis=0, concat_axis=0, tiled=True),
        lax.all_to_all(send_cot, "node", split_axis=0, concat_axis=0, tiled=True),
    )
    weight_gate = w_gate[0]
    weight_up = w_up[0]
    weight_down = w_down[0]
    full_tok, full_cot = (
        lax.all_gather(recv_tok, "local", axis=2, tiled=True),
        lax.all_gather(recv_cot, "local", axis=2, tiled=True),
    )
    flat_tok = full_tok.reshape(row_total, -1)
    flat_cot = full_cot.reshape(row_total, -1)
    gate_pre = jnp.dot(flat_tok, weight_gate, preferred_element_type=jnp.float32)
    up_pre = jnp.dot(flat_tok, weight_up, preferred_element_type=jnp.float32)
    grad_hidden = jnp.einsum("rd,fd->rf", flat_cot, weight_down, preferred_element_type=jnp.float32)
    hidden, grad_gate, grad_up = swiglu_parts(gate_pre, up_pre, grad_hidden)
    output_part = jnp.einsum("fc,rf->cr", weight_down, hidden, preferred_element_type=jnp.float32)
    input_part = jnp.einsum("cf,rf->cr", weight_gate, grad_gate, preferred_element_type=jnp.float32)
    input_part = input_part + jnp.einsum(
        "cf,rf->cr", weight_up, grad_up, preferred_element_type=jnp.float32
    )
    summed = lax.psum_scatter(
        jnp.concatenate([output_part, input_part], axis=1).astype(jnp.bfloat16),
        "local",
        scatter_dimension=0,
        tiled=True,
    )
    outgoing = summed.reshape(width_local, 2, experts, capacity)
    returned = lax.all_to_all(outgoing, "node", split_axis=2, concat_axis=2, tiled=True)
    returned_float = returned.astype(jnp.float32)
    gate_table = jnp.sum(combine_weights[:, :, None] * matches.astype(jnp.float32), axis=1)
    weighted = select_float * gate_table.T[:, None, :]
    layer_out = jnp.einsum("epi,cep->ic", weighted, returned_float[:, 0]).astype(jnp.bfloat16)
    token_grad = jnp.einsum("epi,cep->ic", weighted, returned_float[:, 1]).astype(jnp.bfloat16)
    slot_inner = jnp.einsum("cep,epc->ep", returned_float[:, 0], send_cot.astype(jnp.float32))
    inner = jnp.einsum("epi,ep->ie", select_float, slot_inner)
    partial_grad = jnp.sum(inner[:, None, :] * matches.astype(jnp.float32), axis=2)
    weight_grad = lax.psum(partial_grad, "local")
    return (layer_out, token_grad, weight_grad)


MESH = pl.DeviceIdType.MESH
NT = (((1,), (1,)), ((), ()))
NN = (((1,), (0,)), ((), ()))


def mm(a, b, dims):
    return lax.dot_general(a, b, dims, preferred_element_type=jnp.float32)


def fold(x):
    half = x.shape[-1] // 2
    return jnp.concatenate([x[..., :half], x[..., half:]], axis=-2)


def unfold(x):
    half = x.shape[-2] // 2
    return jnp.concatenate([x[..., :half, :], x[..., half:, :]], axis=-1)


def fused_kernel(
    nodes,
    tok_hbm,
    cot_hbm,
    ids_hbm,
    cw_hbm,
    wg_hbm,
    wu_hbm,
    wd_hbm,
    lo_ref,
    tg_ref,
    wgrad_ref,
    tok_ref,
    cot_ref,
    ids_ref,
    cw_ref,
    wg_v,
    wu_v,
    wd_v,
    xb,
    gt,
    rl,
    rn_s,
    rn,
    mate_s,
    mate_r,
    y_s,
    y_r,
    n_s,
    n_r,
    part,
    in_sem,
    w_sem,
    xs_sem,
    xr_sem,
    gs_sem,
    gr_sem,
    ls_sem,
    lr_sem,
    ns_sem,
    nr_sem,
    ms_sem,
    mr_sem,
    ys_sem,
    yr_sem,
    os_sem,
    or_sem,
):
    me = lax.axis_index("node")
    l = lax.axis_index("local")
    core = lax.rem(l, 2)
    mate = l + 1 - 2 * core
    ymate = lax.rem(l + 2, 4)
    diag = lax.rem(mate + 2, 4)
    order = (l, mate, ymate, diag)
    toks, width = tok_ref.shape
    rows = nodes * toks

    def peer(d):
        return lax.rem(me + d, nodes)

    def source(d):
        return lax.rem(me - d + nodes, nodes)

    in_copies = []
    in_pairs = ((tok_hbm, tok_ref), (cot_hbm, cot_ref), (ids_hbm, ids_ref), (cw_hbm, cw_ref))
    for j, (far, near) in enumerate(in_pairs):
        in_copies.append(pltpu.make_async_copy(far, near, in_sem.at[j]))
        in_copies[j].start()

    barrier = pltpu.get_barrier_semaphore()
    for d in range(1, nodes):
        pl.semaphore_signal(barrier, inc=1, device_id=(peer(d), l), device_id_type=MESH)
    for c in (mate, ymate, diag):
        pl.semaphore_signal(barrier, inc=1, device_id=(me, c), device_id_type=MESH)

    w_copies = []
    for j, c in enumerate(order):
        cols = pl.ds(pl.multiple_of(c * width, width), width)
        group = (
            pltpu.make_async_copy(wg_hbm.at[0, cols, :], wg_v.at[c], w_sem.at[0, j]),
            pltpu.make_async_copy(wu_hbm.at[0, cols, :], wu_v.at[c], w_sem.at[1, j]),
            pltpu.make_async_copy(wd_hbm.at[0, :, cols], wd_v.at[c], w_sem.at[2, j]),
        )
        for copy in group:
            copy.start()
        w_copies.append(group)

    for copy in in_copies:
        copy.wait()
    for kind, ref in enumerate((tok_ref, cot_ref)):
        xb[kind, l, me] = fold(ref[...].astype(jnp.float32)).astype(jnp.bfloat16)
    ids = ids_ref[...]
    lanes = lax.broadcasted_iota(jnp.int32, (toks, 128), 1)
    table = jnp.zeros((toks, 128), jnp.float32)
    for k in range(ids.shape[1]):
        table = table + jnp.where(lanes == ids[:, k : k + 1], cw_ref[:, k : k + 1], 0.0)
    gt[me] = table

    pl.semaphore_wait(barrier, nodes + 2)

    sends = []

    def send(src, dst, ssem, rsem, device):
        copy = pltpu.make_async_remote_copy(
            src_ref=src,
            dst_ref=dst,
            send_sem=ssem,
            recv_sem=rsem,
            device_id=device,
            device_id_type=MESH,
        )
        copy.start()
        sends.append(copy)
        return copy

    x_node = {}
    x_mate, x_y, x_diag = {}, {}, {}

    def outward(kind):
        for d in range(1, nodes):
            block, q = xb.at[kind, l, me], 4 * kind
            x_node[kind, d] = send(block, block, xs_sem.at[q, d], xr_sem.at[q, d], (peer(d), l))

    def onward(kind, d):
        if d:
            x_node[kind, d].wait_recv()
        block, q = xb.at[kind, l, source(d)], 4 * kind + 1
        x_y[kind, d] = send(block, block, xs_sem.at[q, d], xr_sem.at[q, d], (me, ymate))

    def inward(kind):
        block, q = xb.at[kind, l], 4 * kind + 2
        x_mate[kind] = send(block, block, xs_sem.at[q, 0], xr_sem.at[q, 0], (me, mate))

    def relay(kind):
        for d in range(nodes):
            x_y[kind, d].wait_recv()
        block, q = xb.at[kind, ymate], 4 * kind + 3
        x_diag[kind] = send(block, block, xs_sem.at[q, 0], xr_sem.at[q, 0], (me, mate))

    outward(0)
    onward(0, 0)
    outward(1)
    g_node = [None]
    for d in range(1, nodes):
        g_node.append(send(gt.at[me], gt.at[me], gs_sem.at[d], gr_sem.at[d], (peer(d), l)))
    for d in range(1, nodes):
        onward(0, d)
    inward(0)
    for d in range(nodes):
        onward(1, d)
    inward(1)

    def features(kind, c):
        whole = unfold(xb[kind, c].astype(jnp.float32))
        return whole.reshape(rows, width).astype(jnp.bfloat16)

    def arrived(kind, j):
        if j == 1:
            x_mate[kind].wait_recv()
        if j == 3:
            x_diag[kind].wait_recv()

    gate_pre = up_pre = grad_hidden = None
    for j, c in enumerate(order):
        for copy in w_copies[j]:
            copy.wait()
        if j == 1:
            relay(0)
        arrived(0, j)
        tok = features(0, c)
        a = mm(tok, wg_v[c], NN)
        b = mm(tok, wu_v[c], NN)
        if j == 0:
            gate_pre, up_pre = a, b
        else:
            gate_pre, up_pre = gate_pre + a, up_pre + b

    for copy in g_node[1:]:
        copy.wait_recv()
    lanes3 = lax.broadcasted_iota(jnp.int32, (nodes, toks, 128), 2)
    scale = jnp.sum(jnp.where(lanes3 == me, gt[...], 0.0), axis=2, keepdims=True).reshape(rows, 1)
    sigmoid = jax.nn.sigmoid(gate_pre)
    activated = gate_pre * sigmoid
    hidden = activated * up_pre
    hid = (hidden * scale).astype(jnp.bfloat16)

    def partial_out(c):
        return fold(mm(hid, wd_v[c], NN).reshape(nodes, toks, width))

    turns = list(range(1, nodes)) + [0]
    y_copies, o_node, totals = {}, {}, {}

    def to_mate(kind, i, value):
        q = 2 * kind + i
        mate_s[q] = value.astype(jnp.bfloat16)
        return send(mate_s.at[q], mate_r.at[q], ms_sem.at[q], mr_sem.at[q], (me, mate))

    def to_ymate(kind, value, first):
        part[kind] = value
        first.wait_recv()
        y_s[kind] = (part[kind] + mate_r[2 * kind].astype(jnp.float32)).astype(jnp.bfloat16)
        for d in turns:
            n = peer(d)
            y_copies[kind, d] = send(
                y_s.at[kind, n], y_r.at[kind, n], ys_sem.at[kind, d], yr_sem.at[kind, d], (me, ymate)
            )

    def to_nodes(kind, second):
        second.wait_recv()
        for d in turns:
            n = peer(d)
            y_copies[kind, d].wait_recv()
            value = part[kind, n] + mate_r[2 * kind + 1, n].astype(jnp.float32)
            value = value + y_r[kind, n].astype(jnp.float32)
            if d:
                n_s[kind, d] = value.astype(jnp.bfloat16)
                o_node[kind, d] = send(
                    n_s.at[kind, d], n_r.at[kind, me], os_sem.at[kind, d], or_sem.at[kind, d], (n, l)
                )
            else:
                totals[kind] = value

    first = to_mate(0, 0, partial_out(diag))
    to_ymate(0, partial_out(ymate), first)
    second_out = to_mate(0, 1, partial_out(mate))
    part[0] = partial_out(l)
    relay(1)

    for j, c in enumerate(order):
        arrived(1, j)
        g = mm(features(1, c), wd_v[c], NT)
        grad_hidden = g if j == 0 else grad_hidden + g
    inner = jnp.sum(hidden * grad_hidden, axis=1, keepdims=True).reshape(nodes, toks, 1)
    nodes3 = lax.broadcasted_iota(jnp.int32, (nodes, toks, 128), 0)
    rl[l] = jnp.sum(jnp.where(lanes3 == nodes3, inner, 0.0), axis=0)
    r_local = []
    for j, c in enumerate((mate, ymate, diag)):
        r_local.append(send(rl.at[l], rl.at[l], ls_sem.at[j], lr_sem.at[j], (me, c)))
    slope = sigmoid * (1.0 + gate_pre * (1.0 - sigmoid))
    scaled = grad_hidden * scale
    ggate = (scaled * up_pre * slope).astype(jnp.bfloat16)
    gup = (scaled * activated).astype(jnp.bfloat16)

    def partial_in(c):
        value = mm(ggate, wg_v[c], NT) + mm(gup, wu_v[c], NT)
        return fold(value.reshape(nodes, toks, width))

    first = to_mate(1, 0, partial_in(diag))
    to_ymate(1, partial_in(ymate), first)
    second_in = to_mate(1, 1, partial_in(mate))
    to_nodes(0, second_out)
    part[1] = partial_in(l)

    for copy in r_local:
        copy.wait_recv()
    r_sum = rl[0] + rl[1] + rl[2] + rl[3]
    r_node = []
    for d in turns:
        n = peer(d)
        column = jnp.sum(jnp.where(lanes == n, r_sum, 0.0), axis=1, keepdims=True)
        rn_s[d] = jnp.where(lanes == me, column, 0.0)
        if d:
            r_node.append(send(rn_s.at[d], rn.at[me], ns_sem.at[d], nr_sem.at[d], (n, l)))

    to_nodes(1, second_in)
    r_total = rn_s[0]
    for i, d in enumerate(range(1, nodes)):
        r_node[i].wait_recv()
        r_total = r_total + rn[source(d)]
    answer = jnp.zeros(ids.shape, jnp.float32)
    slots = lax.broadcasted_iota(jnp.int32, ids.shape, 1)
    for k in range(ids.shape[1]):
        value = jnp.sum(jnp.where(lanes == ids[:, k : k + 1], r_total, 0.0), axis=1, keepdims=True)
        answer = answer + jnp.where(slots == k, value, 0.0)
    wgrad_ref[...] = answer
    for kind, ref in enumerate((lo_ref, tg_ref)):
        total = totals[kind]
        for d in range(1, nodes):
            o_node[kind, d].wait_recv()
            total = total + n_r[kind, source(d)].astype(jnp.float32)
        ref[...] = unfold(total).astype(jnp.bfloat16)
    for copy in sends:
        copy.wait_send()


def write_kernel(a_ref, b_ref, c_ref, x_ref, y_ref, z_ref):
    x_ref[...] = a_ref[...]
    y_ref[...] = b_ref[...]
    z_ref[...] = c_ref[...]


def fused_body(tokens, cotangent, expert_ids, combine_weights, w_gate, w_up, w_down):
    nodes = lax.axis_size("node")
    toks, width = tokens.shape
    units = w_gate.shape[2]
    half, single = jnp.bfloat16, jnp.float32
    block = (nodes, 2 * toks, width // 2)
    dma = pltpu.SemaphoreType.DMA
    vmem = pl.BlockSpec(memory_space=pltpu.VMEM)
    hbm = pl.BlockSpec(memory_space=pltpu.HBM)
    shapes = (
        jax.ShapeDtypeStruct((toks, width), half),
        jax.ShapeDtypeStruct((toks, width), half),
        jax.ShapeDtypeStruct(expert_ids.shape, single),
    )
    results = pl.pallas_call(
        functools.partial(fused_kernel, nodes),
        out_shape=shapes,
        in_specs=[hbm] * 7,
        out_specs=(vmem, vmem, vmem),
        scratch_shapes=[
            pltpu.VMEM((toks, width), half),
            pltpu.VMEM((toks, width), half),
            pltpu.VMEM(expert_ids.shape, jnp.int32),
            pltpu.VMEM(combine_weights.shape, single),
            pltpu.VMEM((4, width, units), half),
            pltpu.VMEM((4, width, units), half),
            pltpu.VMEM((4, units, width), half),
            pltpu.VMEM((2, 4) + block, half),
            pltpu.VMEM((nodes, toks, 128), single),
            pltpu.VMEM((4, toks, 128), single),
            pltpu.VMEM((nodes, toks, 128), single),
            pltpu.VMEM((nodes, toks, 128), single),
            pltpu.VMEM((4,) + block, half),
            pltpu.VMEM((4,) + block, half),
            pltpu.VMEM((2,) + block, half),
            pltpu.VMEM((2,) + block, half),
            pltpu.VMEM((2,) + block, half),
            pltpu.VMEM((2,) + block, half),
            pltpu.VMEM((2,) + block, single),
            dma((4,)),
            dma((3, 4)),
            dma((8, nodes)),
            dma((8, nodes)),
            dma((nodes,)),
            dma((nodes,)),
            dma((3,)),
            dma((3,)),
            dma((nodes,)),
            dma((nodes,)),
            dma((4,)),
            dma((4,)),
            dma((2, nodes)),
            dma((2, nodes)),
            dma((2, nodes)),
            dma((2, nodes)),
        ],
        compiler_params=pltpu.CompilerParams(
            collective_id=0, has_side_effects=True, vmem_limit_bytes=62 * 1024 * 1024
        ),
    )(tokens, cotangent, expert_ids, combine_weights, w_gate, w_up, w_down)
    return pl.pallas_call(
        write_kernel, out_shape=shapes, in_specs=[vmem] * 3, out_specs=(vmem, vmem, vmem)
    )(*results)


def body(tokens, cotangent, expert_ids, combine_weights, w_gate, w_up, w_down):
    experts = lax.axis_size("node")
    node_tokens = tokens.shape[0]
    top_count = expert_ids.shape[1]
    capacity = min(node_tokens, (3 * node_tokens * top_count + 2 * experts - 1) // (2 * experts))
    whole = capacity == node_tokens and node_tokens == 8 and experts <= 128
    chosen = fused_body if whole and lax.axis_size("local") == 4 else general_body
    return chosen(tokens, cotangent, expert_ids, combine_weights, w_gate, w_up, w_down)


def solution(mesh):
    in_specs = (
        P("node", "local"),
        P("node", "local"),
        P("node", None),
        P("node", None),
        P("node", None, "local"),
        P("node", None, "local"),
        P("node", "local", None),
    )
    out_specs = (P("node", "local"), P("node", "local"), P("node", None))
    return jax.shard_map(body, mesh=mesh, in_specs=in_specs, out_specs=out_specs, check_vma=False)
```

```python
import functools

import jax
import jax.numpy as jnp
from jax import lax
from jax.experimental import pallas as pl
from jax.experimental.pallas import tpu as pltpu
from jax.sharding import PartitionSpec as P


def swiglu_parts(gate_pre, up_pre, grad_hidden):
    sigmoid = jax.nn.sigmoid(gate_pre)
    activated = gate_pre * sigmoid
    hidden = (activated * up_pre).astype(jnp.bfloat16)
    slope = sigmoid * (1.0 + gate_pre * (1.0 - sigmoid))
    grad_gate = (grad_hidden * up_pre * slope).astype(jnp.bfloat16)
    grad_up = (grad_hidden * activated).astype(jnp.bfloat16)
    return (hidden, grad_gate, grad_up)


def general_body(tokens, cotangent, expert_ids, combine_weights, w_gate, w_up, w_down):
    experts = lax.axis_size("node")
    node_tokens, width_local = tokens.shape
    top_count = expert_ids.shape[1]
    capacity = min(node_tokens, (3 * node_tokens * top_count + 2 * experts - 1) // (2 * experts))
    row_total = experts * capacity
    matches = (expert_ids[:, :, None] == lax.iota(jnp.int32, experts)[None, None, :]).astype(
        jnp.int32
    )
    routed = jnp.sum(matches, axis=1)
    position = jnp.cumsum(routed, axis=0) - routed
    kept = routed * (position < capacity).astype(jnp.int32)
    slot_ids = lax.iota(jnp.int32, capacity)
    select_mask = (kept.T[:, None, :] == 1) & (position.T[:, None, :] == slot_ids[None, :, None])
    select_float = select_mask.astype(jnp.float32)
    select_half = select_mask.astype(jnp.bfloat16)
    send_tok = jnp.einsum(
        "epi,id->epd", select_half, tokens, preferred_element_type=jnp.float32
    ).astype(jnp.bfloat16)
    send_cot = jnp.einsum(
        "epi,id->epd", select_half, cotangent, preferred_element_type=jnp.float32
    ).astype(jnp.bfloat16)
    recv_tok, recv_cot = (
        lax.all_to_all(send_tok, "node", split_axis=0, concat_axis=0, tiled=True),
        lax.all_to_all(send_cot, "node", split_axis=0, concat_axis=0, tiled=True),
    )
    weight_gate = w_gate[0]
    weight_up = w_up[0]
    weight_down = w_down[0]
    full_tok, full_cot = (
        lax.all_gather(recv_tok, "local", axis=2, tiled=True),
        lax.all_gather(recv_cot, "local", axis=2, tiled=True),
    )
    flat_tok = full_tok.reshape(row_total, -1)
    flat_cot = full_cot.reshape(row_total, -1)
    gate_pre = jnp.dot(flat_tok, weight_gate, preferred_element_type=jnp.float32)
    up_pre = jnp.dot(flat_tok, weight_up, preferred_element_type=jnp.float32)
    grad_hidden = jnp.einsum("rd,fd->rf", flat_cot, weight_down, preferred_element_type=jnp.float32)
    hidden, grad_gate, grad_up = swiglu_parts(gate_pre, up_pre, grad_hidden)
    output_part = jnp.einsum("fc,rf->cr", weight_down, hidden, preferred_element_type=jnp.float32)
    input_part = jnp.einsum("cf,rf->cr", weight_gate, grad_gate, preferred_element_type=jnp.float32)
    input_part = input_part + jnp.einsum(
        "cf,rf->cr", weight_up, grad_up, preferred_element_type=jnp.float32
    )
    summed = lax.psum_scatter(
        jnp.concatenate([output_part, input_part], axis=1).astype(jnp.bfloat16),
        "local",
        scatter_dimension=0,
        tiled=True,
    )
    outgoing = summed.reshape(width_local, 2, experts, capacity)
    returned = lax.all_to_all(outgoing, "node", split_axis=2, concat_axis=2, tiled=True)
    returned_float = returned.astype(jnp.float32)
    gate_table = jnp.sum(combine_weights[:, :, None] * matches.astype(jnp.float32), axis=1)
    weighted = select_float * gate_table.T[:, None, :]
    layer_out = jnp.einsum("epi,cep->ic", weighted, returned_float[:, 0]).astype(jnp.bfloat16)
    token_grad = jnp.einsum("epi,cep->ic", weighted, returned_float[:, 1]).astype(jnp.bfloat16)
    slot_inner = jnp.einsum("cep,epc->ep", returned_float[:, 0], send_cot.astype(jnp.float32))
    inner = jnp.einsum("epi,ep->ie", select_float, slot_inner)
    partial_grad = jnp.sum(inner[:, None, :] * matches.astype(jnp.float32), axis=2)
    weight_grad = lax.psum(partial_grad, "local")
    return (layer_out, token_grad, weight_grad)


MESH = pl.DeviceIdType.MESH
NT = (((1,), (1,)), ((), ()))
NN = (((1,), (0,)), ((), ()))


def mm(a, b, dims):
    return lax.dot_general(a, b, dims, preferred_element_type=jnp.float32)


def fold(x):
    half = x.shape[-1] // 2
    return jnp.concatenate([x[..., :half], x[..., half:]], axis=-2)


def unfold(x):
    half = x.shape[-2] // 2
    return jnp.concatenate([x[..., :half, :], x[..., half:, :]], axis=-1)


def fused_kernel(
    nodes,
    tok_hbm,
    cot_hbm,
    ids_hbm,
    cw_hbm,
    wg_hbm,
    wu_hbm,
    wd_hbm,
    lo_ref,
    tg_ref,
    wgrad_ref,
    tok_ref,
    cot_ref,
    ids_ref,
    cw_ref,
    wg_v,
    wu_v,
    wd_v,
    xb,
    gt,
    rl,
    rn_s,
    rn,
    mate_s,
    mate_r,
    y_s,
    y_r,
    n_s,
    n_r,
    part,
    in_sem,
    w_sem,
    xs_sem,
    xr_sem,
    gs_sem,
    gr_sem,
    ls_sem,
    lr_sem,
    ns_sem,
    nr_sem,
    ms_sem,
    mr_sem,
    ys_sem,
    yr_sem,
    os_sem,
    or_sem,
):
    me = lax.axis_index("node")
    l = lax.axis_index("local")
    core = lax.rem(l, 2)
    mate = l + 1 - 2 * core
    ymate = lax.rem(l + 2, 4)
    diag = lax.rem(mate + 2, 4)
    order = (l, mate, ymate, diag)
    toks, width = tok_ref.shape
    rows = nodes * toks

    def peer(d):
        return lax.rem(me + d, nodes)

    def source(d):
        return lax.rem(me - d + nodes, nodes)

    in_copies = []
    in_pairs = ((tok_hbm, tok_ref), (cot_hbm, cot_ref), (ids_hbm, ids_ref), (cw_hbm, cw_ref))
    for j, (far, near) in enumerate(in_pairs):
        in_copies.append(pltpu.make_async_copy(far, near, in_sem.at[j]))
        in_copies[j].start()

    barrier = pltpu.get_barrier_semaphore()
    for d in range(1, nodes):
        pl.semaphore_signal(barrier, inc=1, device_id=(peer(d), l), device_id_type=MESH)
    for c in (mate, ymate, diag):
        pl.semaphore_signal(barrier, inc=1, device_id=(me, c), device_id_type=MESH)

    w_copies = []
    for j, c in enumerate(order):
        cols = pl.ds(pl.multiple_of(c * width, width), width)
        group = (
            pltpu.make_async_copy(wg_hbm.at[0, cols, :], wg_v.at[c], w_sem.at[0, j]),
            pltpu.make_async_copy(wu_hbm.at[0, cols, :], wu_v.at[c], w_sem.at[1, j]),
            pltpu.make_async_copy(wd_hbm.at[0, :, cols], wd_v.at[c], w_sem.at[2, j]),
        )
        for copy in group:
            copy.start()
        w_copies.append(group)

    for copy in in_copies:
        copy.wait()
    for kind, ref in enumerate((tok_ref, cot_ref)):
        xb[kind, l, me] = fold(ref[...].astype(jnp.float32)).astype(jnp.bfloat16)
    ids = ids_ref[...]
    lanes = lax.broadcasted_iota(jnp.int32, (toks, 128), 1)
    table = jnp.zeros((toks, 128), jnp.float32)
    for k in range(ids.shape[1]):
        table = table + jnp.where(lanes == ids[:, k : k + 1], cw_ref[:, k : k + 1], 0.0)
    gt[me] = table

    pl.semaphore_wait(barrier, nodes + 2)

    sends = []

    def send(src, dst, ssem, rsem, device):
        copy = pltpu.make_async_remote_copy(
            src_ref=src,
            dst_ref=dst,
            send_sem=ssem,
            recv_sem=rsem,
            device_id=device,
            device_id_type=MESH,
        )
        copy.start()
        sends.append(copy)
        return copy

    x_node = {}
    x_mate, x_y, x_diag = {}, {}, {}

    def outward(kind):
        for d in range(1, nodes):
            block, q = xb.at[kind, l, me], 4 * kind
            x_node[kind, d] = send(block, block, xs_sem.at[q, d], xr_sem.at[q, d], (peer(d), l))

    def onward(kind, d):
        if d:
            x_node[kind, d].wait_recv()
        block, q = xb.at[kind, l, source(d)], 4 * kind + 1
        x_y[kind, d] = send(block, block, xs_sem.at[q, d], xr_sem.at[q, d], (me, ymate))

    def inward(kind):
        block, q = xb.at[kind, l], 4 * kind + 2
        x_mate[kind] = send(block, block, xs_sem.at[q, 0], xr_sem.at[q, 0], (me, mate))

    def relay(kind):
        for d in range(nodes):
            x_y[kind, d].wait_recv()
        block, q = xb.at[kind, ymate], 4 * kind + 3
        x_diag[kind] = send(block, block, xs_sem.at[q, 0], xr_sem.at[q, 0], (me, mate))

    outward(0)
    onward(0, 0)
    outward(1)
    g_node = [None]
    for d in range(1, nodes):
        g_node.append(send(gt.at[me], gt.at[me], gs_sem.at[d], gr_sem.at[d], (peer(d), l)))
    for d in range(1, nodes):
        onward(0, d)
    inward(0)
    for d in range(nodes):
        onward(1, d)
    inward(1)

    def features(kind, c):
        whole = unfold(xb[kind, c].astype(jnp.float32))
        return whole.reshape(rows, width).astype(jnp.bfloat16)

    def arrived(kind, j):
        if j == 1:
            x_mate[kind].wait_recv()
        if j == 3:
            x_diag[kind].wait_recv()

    gate_pre = up_pre = grad_hidden = None
    for j, c in enumerate(order):
        for copy in w_copies[j]:
            copy.wait()
        if j == 1:
            relay(0)
        arrived(0, j)
        tok = features(0, c)
        a = mm(tok, wg_v[c], NN)
        b = mm(tok, wu_v[c], NN)
        if j == 0:
            gate_pre, up_pre = a, b
        else:
            gate_pre, up_pre = gate_pre + a, up_pre + b

    for copy in g_node[1:]:
        copy.wait_recv()
    lanes3 = lax.broadcasted_iota(jnp.int32, (nodes, toks, 128), 2)
    scale = jnp.sum(jnp.where(lanes3 == me, gt[...], 0.0), axis=2, keepdims=True).reshape(rows, 1)
    sigmoid = jax.nn.sigmoid(gate_pre)
    activated = gate_pre * sigmoid
    hidden = activated * up_pre
    hid = (hidden * scale).astype(jnp.bfloat16)

    def partial_out(c):
        return fold(mm(hid, wd_v[c], NN).reshape(nodes, toks, width))

    turns = list(range(1, nodes)) + [0]
    y_copies, o_node, totals = {}, {}, {}

    def to_mate(kind, i, value):
        q = 2 * kind + i
        mate_s[q] = value.astype(jnp.bfloat16)
        return send(mate_s.at[q], mate_r.at[q], ms_sem.at[q], mr_sem.at[q], (me, mate))

    def to_ymate(kind, value, first):
        part[kind] = value
        first.wait_recv()
        y_s[kind] = (part[kind] + mate_r[2 * kind].astype(jnp.float32)).astype(jnp.bfloat16)
        for d in turns:
            n = peer(d)
            y_copies[kind, d] = send(
                y_s.at[kind, n], y_r.at[kind, n], ys_sem.at[kind, d], yr_sem.at[kind, d], (me, ymate)
            )

    def to_nodes(kind, second):
        second.wait_recv()
        for d in turns:
            n = peer(d)
            y_copies[kind, d].wait_recv()
            value = part[kind, n] + mate_r[2 * kind + 1, n].astype(jnp.float32)
            value = value + y_r[kind, n].astype(jnp.float32)
            if d:
                n_s[kind, d] = value.astype(jnp.bfloat16)
                o_node[kind, d] = send(
                    n_s.at[kind, d], n_r.at[kind, me], os_sem.at[kind, d], or_sem.at[kind, d], (n, l)
                )
            else:
                totals[kind] = value

    first = to_mate(0, 0, partial_out(diag))
    to_ymate(0, partial_out(ymate), first)
    second_out = to_mate(0, 1, partial_out(mate))
    part[0] = partial_out(l)
    relay(1)

    for j, c in enumerate(order):
        arrived(1, j)
        g = mm(features(1, c), wd_v[c], NT)
        grad_hidden = g if j == 0 else grad_hidden + g
    inner = jnp.sum(hidden * grad_hidden, axis=1, keepdims=True).reshape(nodes, toks, 1)
    nodes3 = lax.broadcasted_iota(jnp.int32, (nodes, toks, 128), 0)
    rl[l] = jnp.sum(jnp.where(lanes3 == nodes3, inner, 0.0), axis=0)
    r_local = []
    for j, c in enumerate((mate, ymate, diag)):
        r_local.append(send(rl.at[l], rl.at[l], ls_sem.at[j], lr_sem.at[j], (me, c)))
    slope = sigmoid * (1.0 + gate_pre * (1.0 - sigmoid))
    scaled = grad_hidden * scale
    ggate = (scaled * up_pre * slope).astype(jnp.bfloat16)
    gup = (scaled * activated).astype(jnp.bfloat16)

    def partial_in(c):
        value = mm(ggate, wg_v[c], NT) + mm(gup, wu_v[c], NT)
        return fold(value.reshape(nodes, toks, width))

    first = to_mate(1, 0, partial_in(diag))
    to_ymate(1, partial_in(ymate), first)
    to_nodes(0, second_out)
    second_in = to_mate(1, 1, partial_in(mate))
    part[1] = partial_in(l)

    for copy in r_local:
        copy.wait_recv()
    r_sum = rl[0] + rl[1] + rl[2] + rl[3]
    r_node = []
    for d in turns:
        n = peer(d)
        column = jnp.sum(jnp.where(lanes == n, r_sum, 0.0), axis=1, keepdims=True)
        rn_s[d] = jnp.where(lanes == me, column, 0.0)
        if d:
            r_node.append(send(rn_s.at[d], rn.at[me], ns_sem.at[d], nr_sem.at[d], (n, l)))

    to_nodes(1, second_in)
    r_total = rn_s[0]
    for i, d in enumerate(range(1, nodes)):
        r_node[i].wait_recv()
        r_total = r_total + rn[source(d)]
    answer = jnp.zeros(ids.shape, jnp.float32)
    slots = lax.broadcasted_iota(jnp.int32, ids.shape, 1)
    for k in range(ids.shape[1]):
        value = jnp.sum(jnp.where(lanes == ids[:, k : k + 1], r_total, 0.0), axis=1, keepdims=True)
        answer = answer + jnp.where(slots == k, value, 0.0)
    wgrad_ref[...] = answer
    for kind, ref in enumerate((lo_ref, tg_ref)):
        total = totals[kind]
        for d in range(1, nodes):
            o_node[kind, d].wait_recv()
            total = total + n_r[kind, source(d)].astype(jnp.float32)
        ref[...] = unfold(total).astype(jnp.bfloat16)
    for copy in sends:
        copy.wait_send()


def write_kernel(a_ref, b_ref, c_ref, x_ref, y_ref, z_ref):
    x_ref[...] = a_ref[...]
    y_ref[...] = b_ref[...]
    z_ref[...] = c_ref[...]


def fused_body(tokens, cotangent, expert_ids, combine_weights, w_gate, w_up, w_down):
    nodes = lax.axis_size("node")
    toks, width = tokens.shape
    units = w_gate.shape[2]
    half, single = jnp.bfloat16, jnp.float32
    block = (nodes, 2 * toks, width // 2)
    dma = pltpu.SemaphoreType.DMA
    vmem = pl.BlockSpec(memory_space=pltpu.VMEM)
    hbm = pl.BlockSpec(memory_space=pltpu.HBM)
    shapes = (
        jax.ShapeDtypeStruct((toks, width), half),
        jax.ShapeDtypeStruct((toks, width), half),
        jax.ShapeDtypeStruct(expert_ids.shape, single),
    )
    results = pl.pallas_call(
        functools.partial(fused_kernel, nodes),
        out_shape=shapes,
        in_specs=[hbm] * 7,
        out_specs=(vmem, vmem, vmem),
        scratch_shapes=[
            pltpu.VMEM((toks, width), half),
            pltpu.VMEM((toks, width), half),
            pltpu.VMEM(expert_ids.shape, jnp.int32),
            pltpu.VMEM(combine_weights.shape, single),
            pltpu.VMEM((4, width, units), half),
            pltpu.VMEM((4, width, units), half),
            pltpu.VMEM((4, units, width), half),
            pltpu.VMEM((2, 4) + block, half),
            pltpu.VMEM((nodes, toks, 128), single),
            pltpu.VMEM((4, toks, 128), single),
            pltpu.VMEM((nodes, toks, 128), single),
            pltpu.VMEM((nodes, toks, 128), single),
            pltpu.VMEM((4,) + block, half),
            pltpu.VMEM((4,) + block, half),
            pltpu.VMEM((2,) + block, half),
            pltpu.VMEM((2,) + block, half),
            pltpu.VMEM((2,) + block, half),
            pltpu.VMEM((2,) + block, half),
            pltpu.VMEM((2,) + block, single),
            dma((4,)),
            dma((3, 4)),
            dma((8, nodes)),
            dma((8, nodes)),
            dma((nodes,)),
            dma((nodes,)),
            dma((3,)),
            dma((3,)),
            dma((nodes,)),
            dma((nodes,)),
            dma((4,)),
            dma((4,)),
            dma((2, nodes)),
            dma((2, nodes)),
            dma((2, nodes)),
            dma((2, nodes)),
        ],
        compiler_params=pltpu.CompilerParams(
            collective_id=0, has_side_effects=True, vmem_limit_bytes=62 * 1024 * 1024
        ),
    )(tokens, cotangent, expert_ids, combine_weights, w_gate, w_up, w_down)
    return pl.pallas_call(
        write_kernel, out_shape=shapes, in_specs=[vmem] * 3, out_specs=(vmem, vmem, vmem)
    )(*results)


def body(tokens, cotangent, expert_ids, combine_weights, w_gate, w_up, w_down):
    experts = lax.axis_size("node")
    node_tokens = tokens.shape[0]
    top_count = expert_ids.shape[1]
    capacity = min(node_tokens, (3 * node_tokens * top_count + 2 * experts - 1) // (2 * experts))
    whole = capacity == node_tokens and node_tokens == 8 and experts <= 128
    chosen = fused_body if whole and lax.axis_size("local") == 4 else general_body
    return chosen(tokens, cotangent, expert_ids, combine_weights, w_gate, w_up, w_down)


def solution(mesh):
    in_specs = (
        P("node", "local"),
        P("node", "local"),
        P("node", None),
        P("node", None),
        P("node", None, "local"),
        P("node", None, "local"),
        P("node", "local", None),
    )
    out_specs = (P("node", "local"), P("node", "local"), P("node", None))
    return jax.shard_map(body, mesh=mesh, in_specs=in_specs, out_specs=out_specs, check_vma=False)
```
